256 devices in a mesh: dp: 16 (over y, z_lo), fsdp: 16 (over z_hi, x, core).
Axes of the slice: x: 4, y: 4, z: 8 (z_hi: 2, z_lo: 4; z = z_hi * 4 + z_lo), core: 2. Of those that a mesh axis runs over, the one named last changes fastest.
Arguments:
- frames: bfloat16 [4096, 32, 1024], P(('dp', 'fsdp')), may hold values from -6 to 6
- target: int32 [4096], P(('dp', 'fsdp')), may hold values from 0 to 15, as said below
- slot: int32 [4096], P(('dp', 'fsdp')), may hold values from 0 to 15, as said below
- valid: int32 [4096], P(('dp', 'fsdp')), may hold values from 1 to 32
- cotangent: bfloat16 [4096, 32, 1024], P(('dp', 'fsdp')), may hold values from -24 to 24
- norm_gain: float32 [1024], replicated, may hold values from 0.1 to 1.9
- w_in: bfloat16 [1024, 2048], P('fsdp'), may hold values from -0.1875 to 0.1875
- w_out: bfloat16 [1024, 2048], P('fsdp'), may hold values from -0.125 to 0.125
Outputs:
- output: bfloat16 [4096, 32, 1024], P(('dp', 'fsdp'))
- grad_in: float32 [1024, 2048], P('fsdp')
- grad_out: float32 [1024, 2048], P('fsdp')
The draws below stay inside these ranges and needn't reach their ends.
Inputs may be any that keep to these rules, and one draw needn't show every extreme that they name: `target`: the 16 blocks of one device go to distinct indices along dp, to devices with the same fsdp index, so each device sends one block to every index along dp and takes exactly 16 blocks. `slot`: the blocks that one device takes have distinct slots.
All inputs are finite; a program needn't handle non-finite values.
Results may differ from the reference program's by a relative error of at most 0.0054.
Values may be sent and summed in bfloat16 or wider, within the bound.
No kernel may reach another device: no remote copies, remote signals or barrier semaphores. Data moves between devices by JAX's collectives and lax.ppermute only.
A program may use at most 128 MiB of HBM per device.

```python
import math
import jax
import jax.numpy as jnp
from jax import lax

D = 1024
H = 2048
BLOCK_T = 32
LOAD = 16
BLOCKS = 4096
TOKENS = 131072
N_DP = 16
N_FSDP = 16


def route_tables(key):
    first, second = jax.random.split(key)
    sends = jax.vmap(lambda k: jax.random.permutation(k, N_DP))(jax.random.split(first, N_DP * N_FSDP))
    sends = sends.reshape(N_DP, N_FSDP, LOAD).astype(jnp.int32)
    orders = jax.vmap(lambda k: jax.random.permutation(k, LOAD))(jax.random.split(second, N_FSDP * N_DP))
    orders = orders.reshape(N_FSDP, N_DP, LOAD).astype(jnp.int32)
    source = jnp.arange(N_DP, dtype=jnp.int32)[:, None, None]
    column = jnp.arange(N_FSDP, dtype=jnp.int32)[None, :, None]
    places = orders[column, sends, source].astype(jnp.int32)
    return (sends.reshape(BLOCKS), places.reshape(BLOCKS))


def draw_target(key, part):
    return route_tables(key)[0]


def draw_slot(key, part):
    return route_tables(key)[1]


def place_ends(values, stream_key, least, largest):
    index_at = [jax.random.randint(jax.random.fold_in(stream_key, axis), (), 0, length) for axis, length in enumerate(values.shape)]
    main_axis = values.shape.index(max(values.shape))
    beside = index_at[:main_axis] + [(index_at[main_axis] + 1) % values.shape[main_axis]] + index_at[main_axis + 1:]
    return values.at[tuple(index_at)].set(least).at[tuple(beside)].set(largest)


def raised(array, key, source, target, shards_of, factor):
    def block_of(dim):
        return (jnp.arange(array.shape[dim]) // (array.shape[dim] // shards_of)).reshape((-1,) + (1,) * (array.ndim - 1 - dim))

    one_side = jax.random.permutation(key, shards_of)[block_of(target)]
    other_side = (block_of(target) + shards_of // 2) % shards_of
    return jnp.where((block_of(source) == one_side) | (block_of(source) == other_side), factor * array, array)


def levels(stream_key, extent, cuts, least, largest):
    loudness, own = 1.0, jax.random.fold_in(stream_key, 6)
    for dim, shards_of in cuts:
        heights = jnp.exp(jax.random.uniform(jax.random.fold_in(own, dim), (shards_of,), jnp.float32, least / len(cuts), largest / len(cuts)))
        loudness = loudness * jnp.repeat(heights, extent[dim] // shards_of).reshape([-1 if axis == dim else 1 for axis in range(len(extent))])
    return loudness


def noise(own_key, dims, deviation, limit, cuts=(), kind=jnp.bfloat16):
    array = deviation * jax.random.normal(own_key, dims, jnp.float32)
    if cuts:
        array = array * levels(own_key, dims, cuts, -0.22, 0.18)
    return jnp.clip(array, -limit, limit).astype(kind)


def heavy_noise(own_key, dims, deviation, bound, shards, heavy, kind=jnp.bfloat16):
    entries = deviation * jax.random.normal(own_key, dims, jnp.float32)
    if shards:
        entries = entries * levels(own_key, dims, shards, -0.22, 0.18)
    return jnp.clip(raised(entries, jax.random.fold_in(own_key, 3), *heavy), -bound, bound).astype(kind)


def setup_inputs(seed: int = 0) -> dict:
    splits = jax.random.split(jax.random.key(seed), 9)
    frames = noise(splits[0], (BLOCKS, BLOCK_T, D), 1.0, 6.0, ((0, 256),))
    target = draw_target(jax.random.fold_in(splits[8], 71), 0)
    slot = draw_slot(jax.random.fold_in(splits[8], 71), 0)
    valid = place_ends(jax.random.randint(splits[3], (BLOCKS,), 1, BLOCK_T + 1), jax.random.fold_in(splits[3], 1), 1, BLOCK_T).astype(jnp.int32)
    cotangent = heavy_noise(splits[4], (BLOCKS, BLOCK_T, D), 1.0, 24.0, ((0, 256),), (0, 2, 256, 6.0))
    norm_gain = jnp.clip(1.0 + 0.18 * jax.random.normal(splits[5], (D,), jnp.float32), 0.1, 1.9)
    w_in = noise(splits[6], (D, H), D ** -0.5, 0.1875, ((0, 16),))
    w_out = noise(splits[7], (D, H), H ** -0.5, 0.125, ((0, 16),))
    return dict(frames=frames, target=target, slot=slot, valid=valid, cotangent=cotangent, norm_gain=norm_gain, w_in=w_in, w_out=w_out)


def silu_grad(pre):
    sig = jax.nn.sigmoid(pre)
    return sig * (1.0 + pre * (1.0 - sig))

def reference(frames, target, slot, valid, cotangent, norm_gain, w_in, w_out):
    order = jnp.arange(BLOCKS, dtype=jnp.int32)
    column = order // LOAD % N_FSDP
    dest = ((target * N_FSDP + column) * LOAD + slot).astype(jnp.int32)
    moved = jnp.zeros_like(frames).at[dest].set(frames)
    moved_valid = jnp.zeros((BLOCKS,), jnp.int32).at[dest].set(valid)
    group_rows = N_FSDP * LOAD * BLOCK_T
    xs = moved.reshape(N_DP, group_rows, D)
    cs = cotangent.reshape(N_DP, group_rows, D)
    position = jnp.arange(BLOCK_T, dtype=jnp.int32)
    keep = (position[None, :] < moved_valid[:, None]).reshape(N_DP, group_rows)

    def step(carry, inputs):
        grad_a, grad_b = carry
        xrow, crow, krow = inputs
        xf = xrow.astype(jnp.float32)
        mean = lax.optimization_barrier(jnp.mean(xf, axis=1, keepdims=True))
        var = lax.optimization_barrier(jnp.mean((xf - mean) ** 2, axis=1, keepdims=True))
        normed = ((xf - mean) * lax.rsqrt(var + 1e-05) * norm_gain).astype(jnp.bfloat16)
        pre = jnp.dot(normed, w_in, preferred_element_type=jnp.float32)
        act = jax.nn.silu(pre).astype(jnp.bfloat16)
        branch = jnp.dot(act, w_out.T, preferred_element_type=jnp.float32)
        out = (xf + 0.5 * branch).astype(jnp.bfloat16)
        half_cot = jnp.where(krow[:, None], crow * 0.5, 0.0).astype(jnp.bfloat16)
        grad_act = jnp.dot(half_cot, w_out, preferred_element_type=jnp.float32)
        grad_pre = (grad_act * silu_grad(pre)).astype(jnp.bfloat16)
        grad_a = grad_a + jnp.dot(normed.T, grad_pre, preferred_element_type=jnp.float32)
        grad_b = grad_b + jnp.dot(half_cot.T, act, preferred_element_type=jnp.float32)
        return ((grad_a, grad_b), out)
    zeros = jnp.zeros((D, H), jnp.float32)
    (grad_a, grad_b), outs = lax.scan(step, (zeros, zeros), (xs, cs, keep))
    scale = 1.0 / math.sqrt(TOKENS)
    return (outs.reshape(BLOCKS, BLOCK_T, D), grad_a * scale, grad_b * scale)
```

```python
import functools
import math

import jax
import jax.numpy as jnp
from jax import lax
from jax.experimental import pallas as pl
from jax.experimental.pallas import tpu as pltpu
from jax.sharding import PartitionSpec as P

BF = jnp.bfloat16
F32 = jnp.float32
SMEM = pl.BlockSpec(memory_space=pltpu.SMEM)
VMEM = pl.BlockSpec(memory_space=pltpu.VMEM)


def call(kernel, outs, *args, scalars=0, scratch=(), flops=0, io=0):
    return pl.pallas_call(
        kernel,
        out_shape=outs,
        in_specs=[SMEM] * scalars + [VMEM] * (len(args) - scalars),
        out_specs=jax.tree.map(lambda _: VMEM, outs),
        scratch_shapes=list(scratch),
        compiler_params=pltpu.CompilerParams(vmem_limit_bytes=56 * 1024 * 1024),
        cost_estimate=pl.CostEstimate(flops=flops, bytes_accessed=io, transcendentals=0),
    )(*args)


def sds(shape, dtype=BF):
    return jax.ShapeDtypeStruct(shape, dtype)


def fs_shift(v, dzh, dx, dc):
    def to(s):
        zh, x, c = s // 8, (s // 2) % 4, s % 2
        return ((zh + dzh) % 2) * 8 + ((x + dx) % 4) * 2 + (c + dc) % 2

    return lax.ppermute(v, "fsdp", [(s, to(s)) for s in range(16)])


def dp_shift(v, dy, dzl):
    def to(s):
        return ((s // 4 + dy) % 4) * 4 + (s % 4 + dzl) % 4

    return lax.ppermute(v, "dp", [(s, to(s)) for s in range(16)])


def rel_block(idx_ref, b):
    x, zh = idx_ref[1], idx_ref[2]
    return lax.rem(b % 4 - x + 4, 4) * 2 + lax.rem(b // 4 + zh, 2)


def order_kernel(j_ref, slot_ref, valid_ref, frames_ref, out_ref):
    lane = lax.broadcasted_iota(jnp.int32, (16, 128), 1)
    for p in range(16):
        j = j_ref[p]
        for b in range(8):
            out_ref[p, b * 32:(b + 1) * 32, :] = frames_ref[j, :, b * 128:(b + 1) * 128]
        both = jnp.where(lane == 0, slot_ref[j], valid_ref[j])
        out_ref[p, 256:272, :] = both.astype(F32).astype(BF)


def norm_kernel(idx_ref, src_ref, valid_ref, rec_ref, gain_ref, cot_ref, out_ref):
    rel = [pl.multiple_of(rel_block(idx_ref, b) * 128, 128) for b in range(8)]
    position = lax.broadcasted_iota(jnp.int32, (32, 1024), 0)
    for k in range(16):
        src = src_ref[k]
        xf = [rec_ref[src, b * 32:(b + 1) * 32, :].astype(F32) for b in range(8)]
        mean = jnp.sum(functools.reduce(jnp.add, xf), axis=1, keepdims=True) * (1.0 / 1024)
        cen = [v - mean for v in xf]
        var = jnp.sum(functools.reduce(jnp.add, [v * v for v in cen]), axis=1, keepdims=True) * (1.0 / 1024)
        inv = lax.rsqrt(var + 1e-05)
        half = cot_ref[k].astype(F32) * 0.5
        half = jnp.where(position < valid_ref[k], half, 0.0).astype(BF)
        for b in range(8):
            lanes = slice(b * 128, (b + 1) * 128)
            out_ref[0, k * 32:(k + 1) * 32, pl.ds(rel[b], 128)] = (cen[b] * inv * gain_ref[:, lanes]).astype(BF)
            out_ref[1, k * 32:(k + 1) * 32, pl.ds(rel[b], 128)] = half[:, lanes]


def main_kernel(idx_ref, mine, peer, *refs):
    pieces, rest = refs[:10], refs[10:]
    (act, wout, gp, b0, b1, b2, b3, win) = rest
    y = idx_ref[0]
    cols = [pl.multiple_of(lax.rem(n - y + 4, 4) * 256, 256) for n in range(4)]

    def place(ref, src, count, dst):
        for n in range(4):
            win[pl.ds(dst, count), pl.ds(cols[n], 256)] = ref[src:src + count, n * 256:(n + 1) * 256]
            wout[pl.ds(dst, count), pl.ds(cols[n], 256)] = ref[
                src:src + count, 1024 + n * 256:1024 + (n + 1) * 256
            ]

    near = [(pieces[0], 0, 0, 128), (pieces[1], 1, 0, 128), (pieces[2], 2, 0, 64), (pieces[3], 2, 64, 64), (pieces[4], 3, 0, 128)]
    for ref, k, row, count in near:
        place(ref, 0, count, k * 256 + row)
    far = [(pieces[5], 0, 0, 4), (pieces[6], 1, 0, 4), (pieces[7], 2, 0, 2), (pieces[8], 2, 2, 2), (pieces[9], 3, 0, 4)]
    for ref, k, first, count in far:
        for j in range(count):
            at = lax.rem(y + first + j, 4) * 32
            place(ref, j * 32, 32, pl.multiple_of(k * 256 + 128 + at, 32))

    for t in range(4):
        src = mine if t < 2 else peer
        rows = slice((t % 2) * 256, (t % 2) * 256 + 256)
        xv, hv = src[0, rows, :], src[1, rows, :]
        for n in range(4):
            part = slice(n * 256, (n + 1) * 256)
            pre = jnp.dot(xv, win[:, part], preferred_element_type=F32)
            ga = jnp.dot(hv, wout[:, part], preferred_element_type=F32)
            sig = 1.0 / (1.0 + jnp.exp(-pre))
            act[t * 256:(t + 1) * 256, part] = (pre * sig).astype(BF)
            gp[t * 256:(t + 1) * 256, part] = (ga * (sig * (1.0 + pre * (1.0 - sig)))).astype(BF)

    for d in range(4):
        part = slice(d * 256, (d + 1) * 256)
        res = token_sum(mine, peer, 1, part, act)
        for j, ref in enumerate((b0, b1, b2, b3)):
            ref[part, :] = res[:, j * 256:(j + 1) * 256].astype(ref.dtype)


def token_sum(mine, peer, which, part, right):
    dims = (((0,), (0,)), ((), ()))
    res = lax.dot_general(mine[which, :, part], right[:512, :], dims, preferred_element_type=F32)
    return res + lax.dot_general(peer[which, :, part], right[512:, :], dims, preferred_element_type=F32)


def grad_in_kernel(mine, peer, gp, a0, a1, a2, a3):
    for d, ref in enumerate((a0, a1, a2, a3)):
        ref[...] = token_sum(mine, peer, 0, slice(d * 256, (d + 1) * 256), gp).astype(ref.dtype)


def branch_kernel(act, wout, own, other):
    dims = (((1,), (1,)), ((), ()))
    for t in range(4):
        rows = slice((t % 2) * 256, (t % 2) * 256 + 256)
        res = lax.dot_general(act[t * 256:(t + 1) * 256, :], wout[...], dims, preferred_element_type=F32)
        if t < 2:
            own[rows, :] = res
        else:
            other[rows, :] = res.astype(BF)


def output_kernel(idx_ref, src_ref, rec_ref, own, other, out_ref):
    rel = [pl.multiple_of(rel_block(idx_ref, b) * 128, 128) for b in range(8)]
    for k in range(16):
        src = src_ref[k]
        rows = slice(k * 32, (k + 1) * 32)
        for b in range(8):
            branch = own[rows, pl.ds(rel[b], 128)] + other[rows, pl.ds(rel[b], 128)].astype(F32)
            moved = rec_ref[src, b * 32:(b + 1) * 32, :].astype(F32)
            out_ref[k, :, b * 128:(b + 1) * 128] = (moved + 0.5 * branch).astype(BF)


def sum_a(own, r1, r2, r3, o0, o1, o2, o3):
    for j, o in enumerate((o0, o1, o2, o3)):
        part = slice(j * 256, (j + 1) * 256)
        o[...] = (
            own[:, part] + r1[:, part].astype(F32) + r2[:, part].astype(F32) + r3[:, part].astype(F32)
        ).astype(o.dtype)


def sum_b(own, r1, r2, r3, o0, o1, o2, o3):
    for j, o in enumerate((o0, o1, o2, o3)):
        part = slice(j * 256, (j + 1) * 256)
        o[...] = (
            own[part, :] + r1[part, :].astype(F32) + r2[part, :].astype(F32) + r3[part, :].astype(F32)
        ).astype(o.dtype)


def split_kernel(idx_ref, a, a1, a2, a3, b, b1, b2, b3, mine, core, zpair, both):
    c = idx_ref[3]
    for part, refs in enumerate(((a, a1, a2, a3), (b, b1, b2, b3))):
        for h in range(2):
            for d in range(2):
                row = pl.multiple_of(h * 128 + lax.rem(c + d, 2) * 64, 64)
                val = refs[0][pl.ds(row, 64), :]
                for ref in refs[1:]:
                    val = val + ref[pl.ds(row, 64), :].astype(F32)
                dst = ((mine, core), (zpair, both))[h][d]
                dst[part] = val.astype(dst.dtype)


def fold_kernel(mine, core, zpair, both, own, send):
    u = mine[...] + zpair[...].astype(F32)
    v = core[...].astype(F32) + both[...].astype(F32)
    own[0] = u
    own[1] = v
    send[0] = u.astype(BF)
    send[1] = v.astype(BF)


def z_kernel(own, r1, r2, r3, keep, send):
    total = own[...] + r1[...].astype(F32) + r2[...].astype(F32) + r3[...].astype(F32)
    keep[...] = total
    send[...] = total.astype(BF)


def final_kernel(scale, idx_ref, own, r1, r2, r3, g_in, g_out):
    y, c = idx_ref[0], idx_ref[3]
    for j, ref in enumerate((own, r1, r2, r3)):
        for d in range(2):
            at = pl.multiple_of(lax.rem(c + d, 2) * 1024 + lax.rem(y + j, 4) * 256, 256)
            g_in[:, pl.ds(at, 256)] = ref[d, 0].astype(F32) * scale
            g_out[:, pl.ds(at, 256)] = ref[d, 1].astype(F32) * scale


def x_gather(piece):
    k1 = fs_shift(piece, 0, -1, 0)
    k3 = fs_shift(piece, 0, 1, 0)
    half = piece.shape[0] // 2
    k2a = fs_shift(k1[:half], 0, -1, 0)
    k2b = fs_shift(k3[half:], 0, 1, 0)
    return [piece, k1, k2a, k2b, k3]


def per_device(frames, target, slot, valid, cotangent, norm_gain, w_in, w_out):
    dp, fs = lax.axis_index("dp"), lax.axis_index("fsdp")
    y, zh, x, c = dp // 4, fs // 8, (fs // 2) % 4, fs % 2
    idx = jnp.stack([y, x, zh, c]).astype(jnp.int32)
    order = jnp.arange(16, dtype=jnp.int32)

    j_of = jnp.sum(jnp.where(target[None, :] == order[:, None], order[None, :], 0), axis=1)
    sending = call(order_kernel, sds((16, 272, 128)), j_of, slot, valid, frames, scalars=3, io=2 << 20)
    received = lax.all_to_all(sending, "dp", split_axis=0, concat_axis=0, tiled=True)
    details = received[:, 256, :2].astype(jnp.int32)
    place = details[:, 0][None, :] == order[:, None]
    src = jnp.sum(jnp.where(place, order[None, :], 0), axis=1)
    moved_valid = jnp.sum(jnp.where(place, details[:, 1][None, :], 0), axis=1)

    def cut(w, which):
        return lax.dynamic_slice(w, (0, which * 1024), (64, 1024))

    kept = jnp.concatenate([cut(w_in, c), cut(w_out, c)], axis=1)
    swapped = fs_shift(jnp.concatenate([cut(w_in, 1 - c), cut(w_out, 1 - c)], axis=1), 0, 0, 1)
    near = jnp.where(
        c == 0, jnp.concatenate([kept, swapped], axis=0), jnp.concatenate([swapped, kept], axis=0)
    )
    quarter = fs_shift(lax.dynamic_slice(near, (y * 32, 0), (32, 2048)), 1, 0, 0)
    far = jnp.concatenate([quarter] + [dp_shift(quarter, -j, 0) for j in (1, 2, 3)], axis=0)
    near_pieces = x_gather(near)
    far_pieces = x_gather(far)

    mine = call(
        norm_kernel, sds((2, 512, 1024)), idx, src, moved_valid, received, norm_gain[None, :], cotangent,
        scalars=3, io=4 << 20,
    )
    peer = fs_shift(mine, 0, 0, 1)

    square = sds((1024, 1024))
    act, wout, gp, *b = call(
        main_kernel,
        [square] * 3 + [sds((1024, 256), F32)] + [sds((1024, 256))] * 3,
        idx, mine, peer, *near_pieces, *far_pieces,
        scalars=1, scratch=[pltpu.VMEM((1024, 1024), BF)], flops=6 << 30, io=24 << 20,
    )
    b = [b[0]] + [dp_shift(b[j], j, 0) for j in (1, 2, 3)]
    a = call(
        grad_in_kernel, [sds((256, 1024), F32)] + [sds((256, 1024))] * 3, mine, peer, gp, flops=2 << 30, io=8 << 20
    )
    a = [a[0]] + [fs_shift(a[j], 0, j, 0) for j in (1, 2, 3)]

    own, other = call(
        branch_kernel, [sds((512, 1024), F32), sds((512, 1024))], act, wout, flops=2 << 30, io=7 << 20
    )
    other = fs_shift(other, 0, 0, 1)
    output = call(output_kernel, sds((16, 32, 1024)), idx, src, received, own, other, scalars=2, io=5 << 20)

    quad = [sds((256, 256), F32)] + [sds((256, 256))] * 3
    a = call(sum_a, quad, *a, io=2 << 20)
    b = call(sum_b, quad, *b, io=2 << 20)
    a = [a[0]] + [dp_shift(a[j], j, 0) for j in (1, 2, 3)]
    b = [b[0]] + [fs_shift(b[j], 0, j, 0) for j in (1, 2, 3)]
    box = sds((2, 64, 256))
    mine, core, zpair, both = call(
        split_kernel, [sds((2, 64, 256), F32), box, box, box], idx, *a, *b, scalars=1, io=1 << 20
    )
    core, zpair, both = fs_shift(core, 0, 0, 1), fs_shift(zpair, 1, 0, 0), fs_shift(both, 1, 0, 1)
    whole = [sds((2, 2, 64, 256), F32), sds((2, 2, 64, 256))]
    keep, send = call(fold_kernel, whole, mine, core, zpair, both, io=1 << 20)
    keep, send = call(z_kernel, whole, keep, *[dp_shift(send, 0, j) for j in (1, 2, 3)], io=1 << 20)
    scale = 1.0 / math.sqrt(512 * 256)
    grad_in, grad_out = call(
        functools.partial(final_kernel, scale),
        [sds((64, 2048), F32)] * 2,
        idx, keep, *[dp_shift(send, -j, 0) for j in (1, 2, 3)],
        scalars=1,
        io=1 << 20,
    )
    return (output, grad_in, grad_out)


def solution(mesh):
    in_specs = (
        P(("dp", "fsdp"), None, None),
        P(("dp", "fsdp")),
        P(("dp", "fsdp")),
        P(("dp", "fsdp")),
        P(("dp", "fsdp"), None, None),
        P(),
        P("fsdp", None),
        P("fsdp", None),
    )
    out_specs = (P(("dp", "fsdp"), None, None), P("fsdp", None), P("fsdp", None))
    return jax.shard_map(
        per_device, mesh=mesh, in_specs=in_specs, out_specs=out_specs, check_vma=False
    )
```

```python
import functools
import math

import jax
import jax.numpy as jnp
from jax import lax
from jax.experimental import pallas as pl
from jax.experimental.pallas import tpu as pltpu
from jax.sharding import PartitionSpec as P

BF = jnp.bfloat16
F32 = jnp.float32
SMEM = pl.BlockSpec(memory_space=pltpu.SMEM)
VMEM = pl.BlockSpec(memory_space=pltpu.VMEM)


def call(kernel, outs, *args, scalars=0, scratch=()):
    return pl.pallas_call(
        kernel,
        out_shape=outs,
        in_specs=[SMEM] * scalars + [VMEM] * (len(args) - scalars),
        out_specs=jax.tree.map(lambda _: VMEM, outs),
        scratch_shapes=list(scratch),
        compiler_params=pltpu.CompilerParams(vmem_limit_bytes=56 * 1024 * 1024),
        cost_estimate=pl.CostEstimate(flops=1, bytes_accessed=1, transcendentals=0),
    )(*args)


def sds(shape, dtype=BF):
    return jax.ShapeDtypeStruct(shape, dtype)


def fs_shift(v, dzh, dx, dc):
    def to(s):
        zh, x, c = s // 8, (s // 2) % 4, s % 2
        return ((zh + dzh) % 2) * 8 + ((x + dx) % 4) * 2 + (c + dc) % 2

    return lax.ppermute(v, "fsdp", [(s, to(s)) for s in range(16)])


def dp_shift(v, dy, dzl):
    def to(s):
        return ((s // 4 + dy) % 4) * 4 + (s % 4 + dzl) % 4

    return lax.ppermute(v, "dp", [(s, to(s)) for s in range(16)])


def rel_block(idx_ref, b):
    x, zh = idx_ref[1], idx_ref[2]
    return lax.rem(b % 4 - x + 4, 4) * 2 + lax.rem(b // 4 + zh, 2)


def prepare_kernel(idx_ref, to_ref, slot_ref, valid_ref, frames_ref, wi, wo, sending, quarter, near, given):
    lane = lax.broadcasted_iota(jnp.int32, (16, 128), 1)
    for j in range(16):
        p = to_ref[j]
        for b in range(8):
            sending[p, b * 32:(b + 1) * 32, :] = frames_ref[j, :, b * 128:(b + 1) * 128]
        both = jnp.where(lane == 0, slot_ref[j], valid_ref[j])
        sending[p, 256:272, :] = both.astype(F32).astype(BF)
    c, row = idx_ref[3], pl.multiple_of(idx_ref[0] * 16, 16)
    for i, w in enumerate((wi, wo)):
        for dst, which in ((near, c), (given, 1 - c)):
            dst[:, i * 1024:(i + 1) * 1024] = w[:, pl.ds(pl.multiple_of(which * 1024, 1024), 1024)]
        quarter[:, i * 2048:(i + 1) * 2048] = w[pl.ds(row, 16), :]


def halve_kernel(idx_ref, q0, q1, q2, q3, far, given):
    c = idx_ref[3]
    for j, q in enumerate((q0, q1, q2, q3)):
        for i in range(2):
            for dst, which in ((far, c), (given, 1 - c)):
                at = pl.multiple_of(i * 2048 + which * 1024, 1024)
                dst[j * 16:(j + 1) * 16, i * 1024:(i + 1) * 1024] = q[:, pl.ds(at, 1024)]


def norm_kernel(idx_ref, src_ref, valid_ref, rec_ref, gain_ref, cot_ref, out_ref):
    rel = [pl.multiple_of(rel_block(idx_ref, b) * 128, 128) for b in range(8)]
    position = lax.broadcasted_iota(jnp.int32, (32, 1024), 0)
    for k in range(16):
        src = src_ref[k]
        xf = [rec_ref[src, b * 32:(b + 1) * 32, :].astype(F32) for b in range(8)]
        mean = jnp.sum(functools.reduce(jnp.add, xf), axis=1, keepdims=True) * (1.0 / 1024)
        cen = [v - mean for v in xf]
        var = jnp.sum(functools.reduce(jnp.add, [v * v for v in cen]), axis=1, keepdims=True) * (1.0 / 1024)
        inv = lax.rsqrt(var + 1e-05)
        half = cot_ref[k].astype(F32) * 0.5
        half = jnp.where(position < valid_ref[k], half, 0.0).astype(BF)
        for b in range(8):
            lanes = slice(b * 128, (b + 1) * 128)
            out_ref[0, k * 32:(k + 1) * 32, pl.ds(rel[b], 128)] = (cen[b] * inv * gain_ref[:, lanes]).astype(BF)
            out_ref[1, k * 32:(k + 1) * 32, pl.ds(rel[b], 128)] = half[:, lanes]


def place(idx_ref, pieces, win, wout):
    y, c = idx_ref[0], idx_ref[3]

    def put(ref, src, count, dst):
        win[pl.ds(dst, count), :] = ref[src:src + count, :1024]
        wout[pl.ds(dst, count), :] = ref[src:src + count, 1024:]

    for k in range(4):
        for d in range(2):
            at = lax.rem(c + d, 2) * 64
            put(pieces[2 * k + d], 0, 64, pl.multiple_of(k * 256 + at, 64))
            for j in range(4):
                row = k * 256 + 128 + at + lax.rem(y + j, 4) * 16
                put(pieces[8 + 2 * k + d], j * 16, 16, pl.multiple_of(row, 16))


def main_kernel(idx_ref, mine, peer, *refs):
    pieces, (own, other, grad, a0, a1, a2, a3, win, wout, act, gp) = refs[:16], refs[16:]
    place(idx_ref, pieces, win, wout)

    for n in range(4):
        part = slice(n * 256, (n + 1) * 256)
        for s, src in enumerate((mine, peer)):
            rows = slice(s * 512, (s + 1) * 512)
            pre = jnp.dot(src[0], win[:, part], preferred_element_type=F32)
            ga = jnp.dot(src[1], wout[:, part], preferred_element_type=F32)
            sig = 1.0 / (1.0 + jnp.exp(-pre))
            act[rows, part] = (pre * sig).astype(BF)
            gp[rows, part] = (ga * (sig * (1.0 + pre * (1.0 - sig)))).astype(BF)

    def token_sum(which, part, right):
        dims = (((0,), (0,)), ((), ()))
        res = lax.dot_general(mine[which, :, part], right[:512, :], dims, preferred_element_type=F32)
        return res + lax.dot_general(peer[which, :, part], right[512:, :], dims, preferred_element_type=F32)

    for d, ref in enumerate((a0, a1, a2, a3)):
        part = slice(d * 256, (d + 1) * 256)
        res = token_sum(1, part, act)
        for n in range(4):
            grad[n, part, :] = res[:, n * 256:(n + 1) * 256].astype(BF)
        ref[...] = token_sum(0, part, gp).astype(ref.dtype)

    dims = (((1,), (1,)), ((), ()))
    for n in range(4):
        part = slice(n * 256, (n + 1) * 256)
        own[:, part] = lax.dot_general(act[:512, :], wout[part, :], dims, preferred_element_type=F32)
        other[:, part] = lax.dot_general(act[512:, :], wout[part, :], dims, preferred_element_type=F32).astype(BF)


def output_kernel(idx_ref, src_ref, rec_ref, own, other, out_ref):
    rel = [pl.multiple_of(rel_block(idx_ref, b) * 128, 128) for b in range(8)]
    for k in range(16):
        src = src_ref[k]
        rows = slice(k * 32, (k + 1) * 32)
        for b in range(8):
            branch = own[rows, pl.ds(rel[b], 128)] + other[rows, pl.ds(rel[b], 128)].astype(F32)
            moved = rec_ref[src, b * 32:(b + 1) * 32, :].astype(F32)
            out_ref[k, :, b * 128:(b + 1) * 128] = (moved + 0.5 * branch).astype(BF)


def sum_four(ref, rows):
    return sum((ref[j, rows, :].astype(F32) for j in range(1, 4)), ref[0, rows, :].astype(F32))


def sum_kernel(idx_ref, own, r1, r2, r3, parts, *outs):
    for j, o in enumerate(outs[:4]):
        part = pl.ds(pl.multiple_of(lax.rem(idx_ref[0] + j, 4) * 256, 256), 256)
        o[...] = (
            own[:, part] + r1[:, part].astype(F32) + r2[:, part].astype(F32) + r3[:, part].astype(F32)
        ).astype(o.dtype)
    for j, o in enumerate(outs[4:]):
        o[...] = sum_four(parts, slice(j * 256, (j + 1) * 256)).astype(o.dtype)


def split_kernel(idx_ref, a, a1, a2, a3, b, b1, b2, b3, mine, core, zpair, both):
    c = idx_ref[3]
    for part, refs in enumerate(((a, a1, a2, a3), (b, b1, b2, b3))):
        for h in range(2):
            for d in range(2):
                rows = pl.ds(pl.multiple_of(h * 128 + lax.rem(c + d, 2) * 64, 64), 64)
                val = refs[0][rows, :]
                for ref in refs[1:]:
                    val = val + ref[rows, :].astype(F32)
                dst = ((mine, core), (zpair, both))[h][d]
                dst[part] = val.astype(dst.dtype)


def final_kernel(scale, idx_ref, own, r1, r2, r3, g_in, g_out):
    y = idx_ref[0]
    for j, ref in enumerate((own, r1, r2, r3)):
        for d in range(2):
            at = pl.multiple_of(d * 1024 + lax.rem(y + j, 4) * 256, 256)
            g_in[:, pl.ds(at, 256)] = ref[d, 0].astype(F32) * scale
            g_out[:, pl.ds(at, 256)] = ref[d, 1].astype(F32) * scale


def x_sides(piece):
    return fs_shift(piece, 0, -1, 0), fs_shift(piece, 0, 1, 0)


def y_exchange(v):
    groups = [[zl + 4 * y for y in range(4)] for zl in range(4)]
    return lax.all_to_all(v, "dp", split_axis=0, concat_axis=0, axis_index_groups=groups, tiled=True)


def per_device(frames, target, slot, valid, cotangent, norm_gain, w_in, w_out):
    dp, fs = lax.axis_index("dp"), lax.axis_index("fsdp")
    y, zh, x, c = dp // 4, fs // 8, (fs // 2) % 4, fs % 2
    idx = jnp.stack([y, x, zh, c]).astype(jnp.int32)
    order = jnp.arange(16, dtype=jnp.int32)

    barrier = lax.optimization_barrier
    rows64 = sds((64, 2048))
    sending, quarter, near, given = call(
        prepare_kernel, [sds((16, 272, 128)), sds((16, 4096)), rows64, rows64],
        idx, target, slot, valid, frames, w_in, w_out, scalars=4,
    )
    near, near_other, quarter, near_sides = barrier(
        (near, fs_shift(given, 0, 0, 1), fs_shift(quarter, 1, 0, 0), x_sides(near))
    )
    far = [quarter] + [dp_shift(quarter, -j, 0) for j in (1, 2, 3)]
    other_sides = x_sides(near_other)

    sending, far, other_sides = barrier((sending, far, other_sides))
    received = lax.all_to_all(sending, "dp", split_axis=0, concat_axis=0, tiled=True)

    far, given = call(halve_kernel, [rows64, rows64], idx, *far, scalars=1)
    near_across, other_across = fs_shift(near_sides[0], 0, -1, 0), fs_shift(other_sides[1], 0, 1, 0)
    far_other, far_sides = fs_shift(given, 0, 0, 1), x_sides(far)
    near_across, other_across, far_other, far_sides = barrier((near_across, other_across, far_other, far_sides))
    far_other_sides = x_sides(far_other)
    far_across = fs_shift(far_sides[0], 0, -1, 0)
    received, far_across, far_other_sides = barrier((received, far_across, far_other_sides))
    far_other_across = fs_shift(far_other_sides[1], 0, 1, 0)
    pieces = [
        near, near_other, near_sides[0], other_sides[0], near_across, other_across, near_sides[1], other_sides[1],
        far, far_other, far_sides[0], far_other_sides[0], far_across, far_other_across, far_sides[1], far_other_sides[1],
    ]

    details = received[:, 256, :2].astype(jnp.int32)
    place = details[:, 0][None, :] == order[:, None]
    src = jnp.sum(jnp.where(place, order[None, :], 0), axis=1)
    moved_valid = jnp.sum(jnp.where(place, details[:, 1][None, :], 0), axis=1)

    mine = call(
        norm_kernel, sds((2, 512, 1024)), idx, src, moved_valid, received, norm_gain[None, :], cotangent,
        scalars=3,
    )
    mine, far_other_across = barrier((mine, far_other_across))
    pieces[13] = far_other_across
    peer = fs_shift(mine, 0, 0, 1)

    square = pltpu.VMEM((1024, 1024), BF)
    own, other, b, *a = call(
        main_kernel,
        [sds((512, 1024), F32), sds((512, 1024)), sds((4, 1024, 256)), sds((256, 1024), F32)]
        + [sds((256, 1024))] * 3,
        idx, mine, peer, *pieces,
        scalars=1, scratch=[square] * 4,
    )
    b = y_exchange(b)
    a = [a[0]] + [fs_shift(a[j], 0, j, 0) for j in (1, 2, 3)]
    other = fs_shift(other, 0, 0, 1)
    output = call(output_kernel, sds((16, 32, 1024)), idx, src, received, own, other, scalars=2)

    quad = [sds((256, 256), F32)] + [sds((256, 256))] * 3
    b, output, *a = barrier((b, output, *a))
    sums = call(sum_kernel, quad + quad, idx, *a, b, scalars=1)
    a = [sums[0]] + [dp_shift(sums[j], j, 0) for j in (1, 2, 3)]
    b = [sums[4]] + [fs_shift(sums[4 + j], 0, j, 0) for j in (1, 2, 3)]
    box = sds((2, 64, 256))
    split, core, zpair, both = call(
        split_kernel, [sds((2, 64, 256), F32), box, box, box], idx, *a, *b, scalars=1
    )
    core, zpair, both = fs_shift(core, 0, 0, 1), fs_shift(zpair, 1, 0, 0), fs_shift(both, 1, 0, 1)
    mine = split + zpair.astype(F32)
    core = core.astype(F32) + both.astype(F32)
    send = jnp.where(c == 0, jnp.stack([mine, core]), jnp.stack([core, mine])).astype(BF)
    send = sum((dp_shift(send, 0, j).astype(F32) for j in (1, 2, 3)), send.astype(F32)).astype(BF)
    scale = 1.0 / math.sqrt(512 * 256)
    grad_in, grad_out = call(
        functools.partial(final_kernel, scale),
        [sds((64, 2048), F32)] * 2,
        idx, send, *[dp_shift(send, -j, 0) for j in (1, 2, 3)],
        scalars=1,
    )
    return (output, grad_in, grad_out)


def solution(mesh):
    in_specs = (
        P(("dp", "fsdp"), None, None),
        P(("dp", "fsdp")),
        P(("dp", "fsdp")),
        P(("dp", "fsdp")),
        P(("dp", "fsdp"), None, None),
        P(),
        P("fsdp", None),
        P("fsdp", None),
    )
    out_specs = (P(("dp", "fsdp"), None, None), P("fsdp", None), P("fsdp", None))
    return jax.shard_map(
        per_device, mesh=mesh, in_specs=in_specs, out_specs=out_specs, check_vma=False
    )
```

```python
import functools
import math

import jax
import jax.numpy as jnp
from jax import lax
from jax.experimental import pallas as pl
from jax.experimental.pallas import tpu as pltpu
from jax.sharding import PartitionSpec as P

BF = jnp.bfloat16
F32 = jnp.float32
SMEM = pl.BlockSpec(memory_space=pltpu.SMEM)
VMEM = pl.BlockSpec(memory_space=pltpu.VMEM)
ANY = pl.BlockSpec(memory_space=pl.ANY)


def call(kernel, outs, *args, scalars=0, outside=0, scratch=(), space=VMEM):
    return pl.pallas_call(
        kernel,
        out_shape=outs,
        in_specs=[SMEM] * scalars + [ANY] * outside + [VMEM] * (len(args) - scalars - outside),
        out_specs=jax.tree.map(lambda _: space, outs),
        scratch_shapes=list(scratch),
        compiler_params=pltpu.CompilerParams(vmem_limit_bytes=56 * 1024 * 1024),
        cost_estimate=pl.CostEstimate(flops=1, bytes_accessed=1, transcendentals=0),
    )(*args)


def sds(shape, dtype=BF):
    return jax.ShapeDtypeStruct(shape, dtype)


def fs_shift(v, dzh, dx, dc):
    def to(s):
        zh, x, c = s // 8, (s // 2) % 4, s % 2
        return ((zh + dzh) % 2) * 8 + ((x + dx) % 4) * 2 + (c + dc) % 2

    return lax.ppermute(v, "fsdp", [(s, to(s)) for s in range(16)])


def dp_shift(v, dy, dzl):
    def to(s):
        return ((s // 4 + dy) % 4) * 4 + (s % 4 + dzl) % 4

    return lax.ppermute(v, "dp", [(s, to(s)) for s in range(16)])


def rel_block(idx_ref, b):
    x, zh = idx_ref[1], idx_ref[2]
    return lax.rem(b % 4 - x + 4, 4) * 2 + lax.rem(b // 4 + zh, 2)


def prepare_kernel(idx_ref, to_ref, slot_ref, valid_ref, frames_ref, wi, wo, sending, quarter, near, given):
    lane = lax.broadcasted_iota(jnp.int32, (16, 128), 1)
    for j in range(16):
        p = to_ref[j]
        for b in range(8):
            sending[p, b * 32:(b + 1) * 32, :] = frames_ref[j, :, b * 128:(b + 1) * 128]
        both = jnp.where(lane == 0, slot_ref[j], valid_ref[j])
        sending[p, 256:272, :] = both.astype(F32).astype(BF)
    c, row = idx_ref[3], pl.multiple_of(idx_ref[0] * 16, 16)
    for i, w in enumerate((wi, wo)):
        for dst, which in ((near, c), (given, 1 - c)):
            dst[:, i * 1024:(i + 1) * 1024] = w[:, pl.ds(pl.multiple_of(which * 1024, 1024), 1024)]
        quarter[:, i * 2048:(i + 1) * 2048] = w[pl.ds(row, 16), :]


def halve_kernel(idx_ref, q0, q1, q2, q3, far, given):
    c = idx_ref[3]
    for j, q in enumerate((q0, q1, q2, q3)):
        for i in range(2):
            for dst, which in ((far, c), (given, 1 - c)):
                at = pl.multiple_of(i * 2048 + which * 1024, 1024)
                dst[j * 16:(j + 1) * 16, i * 1024:(i + 1) * 1024] = q[:, pl.ds(at, 1024)]


def norm_kernel(idx_ref, src_ref, valid_ref, rec_ref, gain_ref, cot_ref, out_ref):
    rel = [pl.multiple_of(rel_block(idx_ref, b) * 128, 128) for b in range(8)]
    position = lax.broadcasted_iota(jnp.int32, (32, 1024), 0)
    for k in range(16):
        src = src_ref[k]
        xf = [rec_ref[src, b * 32:(b + 1) * 32, :].astype(F32) for b in range(8)]
        mean = jnp.sum(functools.reduce(jnp.add, xf), axis=1, keepdims=True) * (1.0 / 1024)
        cen = [v - mean for v in xf]
        var = jnp.sum(functools.reduce(jnp.add, [v * v for v in cen]), axis=1, keepdims=True) * (1.0 / 1024)
        inv = lax.rsqrt(var + 1e-05)
        half = cot_ref[k].astype(F32) * 0.5
        half = jnp.where(position < valid_ref[k], half, 0.0).astype(BF)
        for b in range(8):
            lanes = slice(b * 128, (b + 1) * 128)
            out_ref[0, k * 32:(k + 1) * 32, pl.ds(rel[b], 128)] = (cen[b] * inv * gain_ref[:, lanes]).astype(BF)
            out_ref[1, k * 32:(k + 1) * 32, pl.ds(rel[b], 128)] = half[:, lanes]


def place(idx_ref, pieces, win, wout):
    y, c = idx_ref[0], idx_ref[3]

    def put(ref, src, count, dst):
        win[pl.ds(dst, count), :] = ref[src:src + count, :1024]
        wout[pl.ds(dst, count), :] = ref[src:src + count, 1024:]

    for k in range(4):
        for d in range(2):
            at = lax.rem(c + d, 2) * 64
            put(pieces[2 * k + d], 0, 64, pl.multiple_of(k * 256 + at, 64))
            for j in range(4):
                row = k * 256 + 128 + at + lax.rem(y + j, 4) * 16
                put(pieces[8 + 2 * k + d], j * 16, 16, pl.multiple_of(row, 16))


def main_kernel(idx_ref, mine, peer, *refs):
    pieces, outs, rest = refs[:16], refs[16:23], refs[23:]
    (win, wout, act, gp, tokens, own, other, grad, a0, a123, sems) = rest
    copies = []

    def send(src, dst):
        copies.append(pltpu.make_async_copy(src, dst, sems.at[len(copies)]))
        copies[-1].start()

    send(mine, tokens.at[0])
    send(peer, tokens.at[1])
    place(idx_ref, pieces, win, wout)

    for s in range(2):
        copies[s].wait()
        rows = slice(s * 512, (s + 1) * 512)
        for n in range(4):
            part = slice(n * 256, (n + 1) * 256)
            pre = jnp.dot(tokens[s, 0], win[:, part], preferred_element_type=F32)
            ga = jnp.dot(tokens[s, 1], wout[:, part], preferred_element_type=F32)
            sig = 1.0 / (1.0 + jnp.exp(-pre))
            act[rows, part] = (pre * sig).astype(BF)
            gp[rows, part] = (ga * (sig * (1.0 + pre * (1.0 - sig)))).astype(BF)

    def token_sum(which, part, right):
        dims = (((0,), (0,)), ((), ()))
        res = lax.dot_general(tokens[0, which, :, part], right[:512, :], dims, preferred_element_type=F32)
        return res + lax.dot_general(tokens[1, which, :, part], right[512:, :], dims, preferred_element_type=F32)

    for d in range(4):
        part = slice(d * 256, (d + 1) * 256)
        res = token_sum(0, part, gp)
        if d == 0:
            a0[...] = res
            send(a0, outs[3])
        else:
            a123[d - 1] = res.astype(BF)
            send(a123.at[d - 1], outs[3 + d])
    for n in range(4):
        part = slice(n * 256, (n + 1) * 256)
        grad[n] = token_sum(1, slice(None), act[:, part]).astype(BF)
        send(grad.at[n], outs[2].at[n])

    dims = (((1,), (1,)), ((), ()))
    for t in range(4):
        rows = slice(t % 2 * 256, t % 2 * 256 + 256)
        res = lax.dot_general(act[t * 256:(t + 1) * 256, :], wout[...], dims, preferred_element_type=F32)
        ref, dst = (own, outs[0]) if t < 2 else (other, outs[1])
        ref[rows, :] = res.astype(ref.dtype)
        send(ref.at[rows], dst.at[rows])
    for copy in copies[2:]:
        copy.wait()


def output_kernel(idx_ref, src_ref, rec_ref, own, other, out_ref):
    rel = [pl.multiple_of(rel_block(idx_ref, b) * 128, 128) for b in range(8)]
    for k in range(16):
        src = src_ref[k]
        rows = slice(k * 32, (k + 1) * 32)
        for b in range(8):
            branch = own[rows, pl.ds(rel[b], 128)] + other[rows, pl.ds(rel[b], 128)].astype(F32)
            moved = rec_ref[src, b * 32:(b + 1) * 32, :].astype(F32)
            out_ref[k, :, b * 128:(b + 1) * 128] = (moved + 0.5 * branch).astype(BF)


def sum_four(ref, rows):
    return sum((ref[j, rows, :].astype(F32) for j in range(1, 4)), ref[0, rows, :].astype(F32))


def sum_kernel(own, r1, r2, r3, parts, a, *outs):
    for j in range(4):
        part = slice(j * 256, (j + 1) * 256)
        a[j] = (
            own[:, part] + r1[:, part].astype(F32) + r2[:, part].astype(F32) + r3[:, part].astype(F32)
        ).astype(BF)
        outs[j][...] = sum_four(parts, part).astype(outs[j].dtype)


def split_kernel(idx_ref, a, b, b1, b2, b3, mine, core, zpair, both):
    c = idx_ref[3]
    for h in range(2):
        for d in range(2):
            rows = pl.ds(pl.multiple_of(h * 128 + lax.rem(c + d, 2) * 64, 64), 64)
            dst = ((mine, core), (zpair, both))[h][d]
            dst[0] = sum_four(a, rows).astype(dst.dtype)
            val = b[rows, :]
            for ref in (b1, b2, b3):
                val = val + ref[rows, :].astype(F32)
            dst[1] = val.astype(dst.dtype)


def final_kernel(scale, idx_ref, own, r1, r2, r3, g_in, g_out):
    y = idx_ref[0]
    for j, ref in enumerate((own, r1, r2, r3)):
        for d in range(2):
            at = pl.multiple_of(d * 1024 + lax.rem(y + j, 4) * 256, 256)
            g_in[:, pl.ds(at, 256)] = ref[d, 0].astype(F32) * scale
            g_out[:, pl.ds(at, 256)] = ref[d, 1].astype(F32) * scale


def x_sides(piece):
    return fs_shift(piece, 0, -1, 0), fs_shift(piece, 0, 1, 0)


def y_exchange(v):
    groups = [[zl + 4 * y for y in range(4)] for zl in range(4)]
    return lax.all_to_all(v, "dp", split_axis=0, concat_axis=0, axis_index_groups=groups, tiled=True)


def per_device(frames, target, slot, valid, cotangent, norm_gain, w_in, w_out):
    dp, fs = lax.axis_index("dp"), lax.axis_index("fsdp")
    y, zh, x, c = dp // 4, fs // 8, (fs // 2) % 4, fs % 2
    idx = jnp.stack([y, x, zh, c]).astype(jnp.int32)
    order = jnp.arange(16, dtype=jnp.int32)

    barrier = lax.optimization_barrier
    rows64 = sds((64, 2048))
    sending, quarter, near, given = call(
        prepare_kernel, [sds((16, 272, 128)), sds((16, 4096)), rows64, rows64],
        idx, target, slot, valid, frames, w_in, w_out, scalars=4,
    )
    near, near_other, quarter, near_sides = barrier(
        (near, fs_shift(given, 0, 0, 1), fs_shift(quarter, 1, 0, 0), x_sides(near))
    )
    far = [quarter] + [dp_shift(quarter, -j, 0) for j in (1, 2, 3)]
    other_sides = x_sides(near_other)

    sending, far, other_sides = barrier((sending, far, other_sides))
    received = lax.all_to_all(sending, "dp", split_axis=0, concat_axis=0, tiled=True)

    far, given = call(halve_kernel, [rows64, rows64], idx, *far, scalars=1)
    near_across, other_across = fs_shift(near_sides[0], 0, -1, 0), fs_shift(other_sides[1], 0, 1, 0)
    far_other, far_sides = fs_shift(given, 0, 0, 1), x_sides(far)
    near_across, other_across, far_other, far_sides = barrier((near_across, other_across, far_other, far_sides))
    far_other_sides = x_sides(far_other)
    far_across = fs_shift(far_sides[0], 0, -1, 0)
    received, far_across, far_other_sides = barrier((received, far_across, far_other_sides))
    far_other_across = fs_shift(far_other_sides[1], 0, 1, 0)
    pieces = [
        near, near_other, near_sides[0], other_sides[0], near_across, other_across, near_sides[1], other_sides[1],
        far, far_other, far_sides[0], far_other_sides[0], far_across, far_other_across, far_sides[1], far_other_sides[1],
    ]

    details = received[:, 256, :2].astype(jnp.int32)
    place = details[:, 0][None, :] == order[:, None]
    src = jnp.sum(jnp.where(place, order[None, :], 0), axis=1)
    moved_valid = jnp.sum(jnp.where(place, details[:, 1][None, :], 0), axis=1)

    mine = call(
        norm_kernel, sds((2, 512, 1024)), idx, src, moved_valid, received, norm_gain[None, :], cotangent,
        scalars=3,
    )
    mine, far_other_across = barrier((mine, far_other_across))
    pieces[13] = far_other_across
    peer = fs_shift(mine, 0, 0, 1)

    square = pltpu.VMEM((1024, 1024), BF)
    own, other, b, *a = call(
        main_kernel,
        [sds((512, 1024), F32), sds((512, 1024)), sds((4, 1024, 256)), sds((256, 1024), F32)]
        + [sds((256, 1024))] * 3,
        idx, mine, peer, *pieces,
        scalars=1,
        outside=2,
        scratch=[square] * 4 + [pltpu.VMEM((2, 2, 512, 1024), BF)]
        + [pltpu.VMEM((512, 1024), F32), pltpu.VMEM((512, 1024), BF), pltpu.VMEM((4, 1024, 256), BF)]
        + [pltpu.VMEM((256, 1024), F32), pltpu.VMEM((3, 256, 1024), BF), pltpu.SemaphoreType.DMA((14,))],
        space=ANY,
    )
    b = y_exchange(b)
    a = [a[0]] + [fs_shift(a[j], 0, j, 0) for j in (1, 2, 3)]
    other = fs_shift(other, 0, 0, 1)
    output = call(output_kernel, sds((16, 32, 1024)), idx, src, received, own, other, scalars=2)

    quad = [sds((256, 256), F32)] + [sds((256, 256))] * 3
    b, output, *a = barrier((b, output, *a))
    a, *b = call(sum_kernel, [sds((4, 256, 256))] + quad, *a, b)
    a = y_exchange(a)
    b = [b[0]] + [fs_shift(b[j], 0, j, 0) for j in (1, 2, 3)]
    box = sds((2, 64, 256))
    split, core, zpair, both = call(
        split_kernel, [sds((2, 64, 256), F32), box, box, box], idx, a, *b, scalars=1
    )
    core, zpair, both = fs_shift(core, 0, 0, 1), fs_shift(zpair, 1, 0, 0), fs_shift(both, 1, 0, 1)
    mine = split + zpair.astype(F32)
    core = core.astype(F32) + both.astype(F32)
    send = jnp.where(c == 0, jnp.stack([mine, core]), jnp.stack([core, mine])).astype(BF)
    send = sum((dp_shift(send, 0, j).astype(F32) for j in (1, 2, 3)), send.astype(F32)).astype(BF)
    scale = 1.0 / math.sqrt(512 * 256)
    grad_in, grad_out = call(
        functools.partial(final_kernel, scale),
        [sds((64, 2048), F32)] * 2,
        idx, send, *[dp_shift(send, -j, 0) for j in (1, 2, 3)],
        scalars=1,
    )
    return (output, grad_in, grad_out)


def solution(mesh):
    in_specs = (
        P(("dp", "fsdp"), None, None),
        P(("dp", "fsdp")),
        P(("dp", "fsdp")),
        P(("dp", "fsdp")),
        P(("dp", "fsdp"), None, None),
        P(),
        P("fsdp", None),
        P("fsdp", None),
    )
    out_specs = (P(("dp", "fsdp"), None, None), P("fsdp", None), P("fsdp", None))
    return jax.shard_map(
        per_device, mesh=mesh, in_specs=in_specs, out_specs=out_specs, check_vma=False
    )
```

```python
import functools
import math

import jax
import jax.numpy as jnp
from jax import lax
from jax.experimental import pallas as pl
from jax.experimental.pallas import tpu as pltpu
from jax.sharding import PartitionSpec as P

BF = jnp.bfloat16
F32 = jnp.float32
SMEM = pl.BlockSpec(memory_space=pltpu.SMEM)
VMEM = pl.BlockSpec(memory_space=pltpu.VMEM)
ANY = pl.BlockSpec(memory_space=pl.ANY)


def call(kernel, outs, *args, scalars=0, outside=0, scratch=(), space=VMEM, limit=56):
    return pl.pallas_call(
        kernel,
        out_shape=outs,
        in_specs=[SMEM] * scalars + [ANY] * outside + [VMEM] * (len(args) - scalars - outside),
        out_specs=jax.tree.map(lambda _: space, outs),
        scratch_shapes=list(scratch),
        compiler_params=pltpu.CompilerParams(vmem_limit_bytes=limit * 1024 * 1024),
        cost_estimate=pl.CostEstimate(flops=1, bytes_accessed=1, transcendentals=0),
    )(*args)


def sds(shape, dtype=BF):
    return jax.ShapeDtypeStruct(shape, dtype)


def fs_shift(v, dzh, dx, dc):
    def to(s):
        zh, x, c = s // 8, (s // 2) % 4, s % 2
        return ((zh + dzh) % 2) * 8 + ((x + dx) % 4) * 2 + (c + dc) % 2

    return lax.ppermute(v, "fsdp", [(s, to(s)) for s in range(16)])


def dp_shift(v, dy, dzl):
    def to(s):
        return ((s // 4 + dy) % 4) * 4 + (s % 4 + dzl) % 4

    return lax.ppermute(v, "dp", [(s, to(s)) for s in range(16)])


def rel_block(idx_ref, b):
    x, zh = idx_ref[1], idx_ref[2]
    return lax.rem(b % 4 - x + 4, 4) * 2 + lax.rem(b // 4 + zh, 2)


def prepare_kernel(idx_ref, to_ref, slot_ref, valid_ref, frames_ref, wi, wo, sending, quarter, near, given):
    lane = lax.broadcasted_iota(jnp.int32, (16, 128), 1)
    for j in range(16):
        p = to_ref[j]
        for b in range(8):
            sending[p, b * 32:(b + 1) * 32, :] = frames_ref[j, :, b * 128:(b + 1) * 128]
        both = jnp.where(lane == 0, slot_ref[j], valid_ref[j])
        sending[p, 256:272, :] = both.astype(F32).astype(BF)
    c, row = idx_ref[3], pl.multiple_of(idx_ref[0] * 16, 16)
    for i, w in enumerate((wi, wo)):
        for dst, which in ((near, c), (given, 1 - c)):
            dst[:, i * 1024:(i + 1) * 1024] = w[:, pl.ds(pl.multiple_of(which * 1024, 1024), 1024)]
        quarter[:, i * 2048:(i + 1) * 2048] = w[pl.ds(row, 16), :]


def halve_kernel(idx_ref, q0, q1, q2, q3, far, given):
    c = idx_ref[3]
    for j, q in enumerate((q0, q1, q2, q3)):
        for i in range(2):
            for dst, which in ((far, c), (given, 1 - c)):
                at = pl.multiple_of(i * 2048 + which * 1024, 1024)
                dst[j * 16:(j + 1) * 16, i * 1024:(i + 1) * 1024] = q[:, pl.ds(at, 1024)]


def norm_kernel(idx_ref, src_ref, valid_ref, rec_ref, gain_ref, cot_ref, out_ref):
    rel = [pl.multiple_of(rel_block(idx_ref, b) * 128, 128) for b in range(8)]
    position = lax.broadcasted_iota(jnp.int32, (32, 1024), 0)
    for k in range(16):
        src = src_ref[k]
        xf = [rec_ref[src, b * 32:(b + 1) * 32, :].astype(F32) for b in range(8)]
        mean = jnp.sum(functools.reduce(jnp.add, xf), axis=1, keepdims=True) * (1.0 / 1024)
        cen = [v - mean for v in xf]
        var = jnp.sum(functools.reduce(jnp.add, [v * v for v in cen]), axis=1, keepdims=True) * (1.0 / 1024)
        inv = lax.rsqrt(var + 1e-05)
        half = cot_ref[k].astype(F32) * 0.5
        half = jnp.where(position < valid_ref[k], half, 0.0).astype(BF)
        for b in range(8):
            lanes = slice(b * 128, (b + 1) * 128)
            out_ref[0, k * 32:(k + 1) * 32, pl.ds(rel[b], 128)] = (cen[b] * inv * gain_ref[:, lanes]).astype(BF)
            out_ref[1, k * 32:(k + 1) * 32, pl.ds(rel[b], 128)] = half[:, lanes]


def place(idx_ref, pieces, win, wout):
    y, c = idx_ref[0], idx_ref[3]

    def put(ref, src, count, dst):
        win[pl.ds(dst, count), :] = ref[src:src + count, :1024]
        wout[pl.ds(dst, count), :] = ref[src:src + count, 1024:]

    for k in range(4):
        for d in range(2):
            at = lax.rem(c + d, 2) * 64
            put(pieces[2 * k + d], 0, 64, pl.multiple_of(k * 256 + at, 64))
            for j in range(4):
                row = k * 256 + 128 + at + lax.rem(y + j, 4) * 16
                put(pieces[8 + 2 * k + d], j * 16, 16, pl.multiple_of(row, 16))


def main_kernel(idx_ref, mine, peer, *refs):
    pieces, outs, rest = refs[:16], refs[16:23], refs[23:]
    (win, wout, act, gp, tokens, own, other, grad, a0, a123, sems) = rest
    copies = []

    def send(src, dst):
        copies.append(pltpu.make_async_copy(src, dst, sems.at[len(copies)]))
        copies[-1].start()

    send(mine, tokens.at[0])
    send(peer, tokens.at[1])
    place(idx_ref, pieces, win, wout)

    for s in range(2):
        copies[s].wait()
        rows = slice(s * 512, (s + 1) * 512)
        for n in range(4):
            part = slice(n * 256, (n + 1) * 256)
            pre = jnp.dot(tokens[s, 0], win[:, part], preferred_element_type=F32)
            ga = jnp.dot(tokens[s, 1], wout[:, part], preferred_element_type=F32)
            sig = 1.0 / (1.0 + jnp.exp(-pre))
            act[rows, part] = (pre * sig).astype(BF)
            gp[rows, part] = (ga * (sig * (1.0 + pre * (1.0 - sig)))).astype(BF)

    def token_sum(which, part, right):
        dims = (((0,), (0,)), ((), ()))
        res = lax.dot_general(tokens[0, which, :, part], right[:512, :], dims, preferred_element_type=F32)
        return res + lax.dot_general(tokens[1, which, :, part], right[512:, :], dims, preferred_element_type=F32)

    for d in range(4):
        part = slice(d * 256, (d + 1) * 256)
        res = token_sum(0, part, gp)
        if d == 0:
            a0[...] = res
            send(a0, outs[3])
        else:
            a123[d - 1] = res.astype(BF)
            send(a123.at[d - 1], outs[3 + d])
    for n in range(4):
        part = slice(n * 256, (n + 1) * 256)
        grad[n] = token_sum(1, slice(None), act[:, part]).astype(BF)
        send(grad.at[n], outs[2].at[n])

    dims = (((1,), (1,)), ((), ()))
    for t in range(4):
        rows = slice(t % 2 * 256, t % 2 * 256 + 256)
        res = lax.dot_general(act[t * 256:(t + 1) * 256, :], wout[...], dims, preferred_element_type=F32)
        ref, dst = (own, outs[0]) if t < 2 else (other, outs[1])
        ref[rows, :] = res.astype(ref.dtype)
        send(ref.at[rows], dst.at[rows])
    for copy in copies[2:]:
        copy.wait()


def output_kernel(idx_ref, src_ref, rec_ref, own, other, out_ref):
    rel = [pl.multiple_of(rel_block(idx_ref, b) * 128, 128) for b in range(8)]
    for k in range(16):
        src = src_ref[k]
        rows = slice(k * 32, (k + 1) * 32)
        for b in range(8):
            branch = own[rows, pl.ds(rel[b], 128)] + other[rows, pl.ds(rel[b], 128)].astype(F32)
            moved = rec_ref[src, b * 32:(b + 1) * 32, :].astype(F32)
            out_ref[k, :, b * 128:(b + 1) * 128] = (moved + 0.5 * branch).astype(BF)


def sum_four(ref, rows):
    return sum((ref[j, rows, :].astype(F32) for j in range(1, 4)), ref[0, rows, :].astype(F32))


def sum_kernel(own, r1, r2, r3, parts, a, *outs):
    for j in range(4):
        part = slice(j * 256, (j + 1) * 256)
        a[j] = (
            own[:, part] + r1[:, part].astype(F32) + r2[:, part].astype(F32) + r3[:, part].astype(F32)
        ).astype(BF)
        outs[j][...] = sum_four(parts, part).astype(outs[j].dtype)


def split_kernel(idx_ref, a, b, b1, b2, b3, mine, core, zpair, both):
    c = idx_ref[3]
    for h in range(2):
        for d in range(2):
            rows = pl.ds(pl.multiple_of(h * 128 + lax.rem(c + d, 2) * 64, 64), 64)
            dst = ((mine, core), (zpair, both))[h][d]
            dst[0] = sum_four(a, rows).astype(dst.dtype)
            val = b[rows, :]
            for ref in (b1, b2, b3):
                val = val + ref[rows, :].astype(F32)
            dst[1] = val.astype(dst.dtype)


def final_kernel(scale, idx_ref, own, r1, r2, r3, g_in, g_out):
    y = idx_ref[0]
    for j, ref in enumerate((own, r1, r2, r3)):
        for d in range(2):
            at = pl.multiple_of(d * 1024 + lax.rem(y + j, 4) * 256, 256)
            g_in[:, pl.ds(at, 256)] = ref[d, 0].astype(F32) * scale
            g_out[:, pl.ds(at, 256)] = ref[d, 1].astype(F32) * scale


def x_sides(piece):
    return fs_shift(piece, 0, -1, 0), fs_shift(piece, 0, 1, 0)


def y_exchange(v):
    groups = [[zl + 4 * y for y in range(4)] for zl in range(4)]
    return lax.all_to_all(v, "dp", split_axis=0, concat_axis=0, axis_index_groups=groups, tiled=True)


def per_device(frames, target, slot, valid, cotangent, norm_gain, w_in, w_out):
    dp, fs = lax.axis_index("dp"), lax.axis_index("fsdp")
    y, zh, x, c = dp // 4, fs // 8, (fs // 2) % 4, fs % 2
    idx = jnp.stack([y, x, zh, c]).astype(jnp.int32)
    order = jnp.arange(16, dtype=jnp.int32)

    barrier = lax.optimization_barrier
    rows64 = sds((64, 2048))
    sending, quarter, near, given = call(
        prepare_kernel, [sds((16, 272, 128)), sds((16, 4096)), rows64, rows64],
        idx, target, slot, valid, frames, w_in, w_out, scalars=4,
    )
    near, near_other, quarter, near_sides = barrier(
        (near, fs_shift(given, 0, 0, 1), fs_shift(quarter, 1, 0, 0), x_sides(near))
    )
    far = [quarter] + [dp_shift(quarter, -j, 0) for j in (1, 2, 3)]
    other_sides = x_sides(near_other)

    sending, far, other_sides = barrier((sending, far, other_sides))
    received = lax.all_to_all(sending, "dp", split_axis=0, concat_axis=0, tiled=True)

    far, given = call(halve_kernel, [rows64, rows64], idx, *far, scalars=1)
    near_across, other_across = fs_shift(near_sides[0], 0, -1, 0), fs_shift(other_sides[1], 0, 1, 0)
    far_other, far_sides = fs_shift(given, 0, 0, 1), x_sides(far)
    near_across, other_across, far_other, far_sides = barrier((near_across, other_across, far_other, far_sides))
    far_other_sides = x_sides(far_other)
    far_across = fs_shift(far_sides[0], 0, -1, 0)
    received, far_across, far_other_sides = barrier((received, far_across, far_other_sides))
    far_other_across = fs_shift(far_other_sides[1], 0, 1, 0)
    pieces = [
        near, near_other, near_sides[0], other_sides[0], near_across, other_across, near_sides[1], other_sides[1],
        far, far_other, far_sides[0], far_other_sides[0], far_across, far_other_across, far_sides[1], far_other_sides[1],
    ]

    details = received[:, 256, :2].astype(jnp.int32)
    place = details[:, 0][None, :] == order[:, None]
    src = jnp.sum(jnp.where(place, order[None, :], 0), axis=1)
    moved_valid = jnp.sum(jnp.where(place, details[:, 1][None, :], 0), axis=1)

    mine = call(
        norm_kernel, sds((2, 512, 1024)), idx, src, moved_valid, received, norm_gain[None, :], cotangent,
        scalars=3,
    )
    mine, far_other_across = barrier((mine, far_other_across))
    pieces[13] = far_other_across
    peer = fs_shift(mine, 0, 0, 1)

    square = pltpu.VMEM((1024, 1024), BF)
    own, other, b, *a = call(
        main_kernel,
        [sds((512, 1024), F32), sds((512, 1024)), sds((4, 1024, 256)), sds((256, 1024), F32)]
        + [sds((256, 1024))] * 3,
        idx, mine, peer, *pieces,
        scalars=1,
        outside=2,
        scratch=[square] * 4 + [pltpu.VMEM((2, 2, 512, 1024), BF)]
        + [pltpu.VMEM((512, 1024), F32), pltpu.VMEM((512, 1024), BF), pltpu.VMEM((4, 1024, 256), BF)]
        + [pltpu.VMEM((256, 1024), F32), pltpu.VMEM((3, 256, 1024), BF), pltpu.SemaphoreType.DMA((14,))],
        space=ANY,
        limit=62,
    )
    b = y_exchange(b)
    a = [a[0]] + [fs_shift(a[j], 0, j, 0) for j in (1, 2, 3)]
    other = fs_shift(other, 0, 0, 1)
    output = call(output_kernel, sds((16, 32, 1024)), idx, src, received, own, other, scalars=2)

    quad = [sds((256, 256), F32)] + [sds((256, 256))] * 3
    b, output, *a = barrier((b, output, *a))
    a, *b = call(sum_kernel, [sds((4, 256, 256))] + quad, *a, b)
    a = y_exchange(a)
    b = [b[0]] + [fs_shift(b[j], 0, j, 0) for j in (1, 2, 3)]
    box = sds((2, 64, 256))
    split, core, zpair, both = call(
        split_kernel, [sds((2, 64, 256), F32), box, box, box], idx, a, *b, scalars=1
    )
    core, zpair, both = fs_shift(core, 0, 0, 1), fs_shift(zpair, 1, 0, 0), fs_shift(both, 1, 0, 1)
    mine = split + zpair.astype(F32)
    core = core.astype(F32) + both.astype(F32)
    send = jnp.where(c == 0, jnp.stack([mine, core]), jnp.stack([core, mine])).astype(BF)
    send = sum((dp_shift(send, 0, j).astype(F32) for j in (1, 2, 3)), send.astype(F32)).astype(BF)
    scale = 1.0 / math.sqrt(512 * 256)
    grad_in, grad_out = call(
        functools.partial(final_kernel, scale),
        [sds((64, 2048), F32)] * 2,
        idx, send, *[dp_shift(send, -j, 0) for j in (1, 2, 3)],
        scalars=1,
    )
    return (output, grad_in, grad_out)


def solution(mesh):
    in_specs = (
        P(("dp", "fsdp"), None, None),
        P(("dp", "fsdp")),
        P(("dp", "fsdp")),
        P(("dp", "fsdp")),
        P(("dp", "fsdp"), None, None),
        P(),
        P("fsdp", None),
        P("fsdp", None),
    )
    out_specs = (P(("dp", "fsdp"), None, None), P("fsdp", None), P("fsdp", None))
    return jax.shard_map(
        per_device, mesh=mesh, in_specs=in_specs, out_specs=out_specs, check_vma=False
    )
```
